32 devices in a mesh: dp: 16 (over z, x, core), sp: 2 (over y).
Axes of the slice: x: 2, y: 2, z: 4, core: 2. Of those that a mesh axis runs over, the one named last changes fastest.
Arguments:
- vision: bfloat16 [16, 128, 8192], P('dp', None, 'sp'), may hold values from -6 to 6
- key_projection_weight: bfloat16 [8192, 1024], P(('sp', 'dp')), may hold values from -0.0625 to 0.0625
- value_projection_weight: bfloat16 [8192, 1024], P(('sp', 'dp')), may hold values from -0.0625 to 0.0625
- key_gain: float32 [128], replicated, may hold values from 0.1 to 1.9
- queries: bfloat16 [16, 256, 4096], P('dp', 'sp'), may hold values from -40 to 40
- out_grad: bfloat16 [16, 256, 4096], P('dp', 'sp'), may hold values from -6 to 6
- image_ids: int32 [16, 16], P('dp'), may hold values from 0 to 15
- image_counts: int32 [16], P('dp'), may hold values from 4 to 16
- image_starts: int32 [16, 16], P('dp'), may hold values from 0 to 255
Outputs:
- attended: bfloat16 [16, 256, 4096], P('dp', 'sp')
- grad_queries: bfloat16 [16, 256, 4096], P('dp', 'sp')
- grad_wkey: float32 [8192, 1024], P(('sp', 'dp'))
- grad_wvalue: float32 [8192, 1024], P(('sp', 'dp'))
The draws below stay inside these ranges and needn't reach their ends.
Inputs may be any that keep to these rules, and one draw needn't show every extreme that they name: `image_starts`: slot 0 is seen by every token whatever its start.
All inputs are finite; a program needn't handle non-finite values.
Results may differ from the reference program's by a relative error of at most 0.015.
The reference program's roundings to bfloat16 on the way count: a program that leaves them out, or rounds other values in their place, can miss the bound.
Values may be sent and summed in bfloat16 or wider, within the bound.
No kernel may reach another device: no remote copies, remote signals or barrier semaphores. Data moves between devices by JAX's collectives and lax.ppermute only.
A program may use at most 128 MiB of HBM per device.

```python
import math
import jax
import jax.numpy as jnp
from jax import lax

MODEL_WIDTH = 8192
KEY_VALUE_HEADS = 8
HEAD_SIZE = 128
HQ = 32
IMAGE_TOKENS = 128
IMAGE_SLOTS = 16
DOCS = 16
LEN = 256
IMAGES_TOTAL = 16


def draw_queries(key, part):
    key = jax.random.fold_in(key, 7)
    first_key = jax.random.fold_in(key, 0)
    drawn_values = jax.random.normal(first_key, (DOCS, LEN, HQ * HEAD_SIZE), jnp.float32)
    return jnp.clip(drawn_values, -40.0, 40.0).astype(jnp.bfloat16)


def place_ends(entries, rng, least, top_value):
    longest = entries.shape.index(max(entries.shape))
    spots = []
    for shift in (0, 1):
        where = [jax.random.randint(jax.random.fold_in(rng, axis), (), 0, length) for axis, length in enumerate(entries.shape)]
        where[longest] = (where[longest] + shift) % entries.shape[longest]
        spots.append(tuple(where))
    return entries.at[spots[0]].set(least).at[spots[1]].set(top_value)


def level_of(key, shape, shards, smallest, high):
    factor_of = 1.0
    for dim, shards_of in shards:
        draws = jax.random.uniform(jax.random.fold_in(jax.random.fold_in(key, 6), dim), (shards_of,), jnp.float32, smallest / len(shards), high / len(shards))
        factor_of = factor_of * jnp.repeat(jnp.exp(draws), shape[dim] // shards_of).reshape((-1,) + (1,) * (len(shape) - 1 - dim))
    return factor_of


def scatter_about(stream_key, dims, spread, limit, pieces=(), kind=jnp.bfloat16):
    values = jax.random.normal(stream_key, dims, jnp.float32) * spread
    if len(pieces) > 0:
        values = level_of(stream_key, dims, pieces, -0.22, 0.18) * values
    return jnp.clip(values, min=-limit, max=limit).astype(kind)


def setup_inputs(seed: int = 0) -> dict:
    key_list = jax.random.split(jax.random.key(seed), 10)
    return {
        "vision": scatter_about(key_list[0], (IMAGES_TOTAL, IMAGE_TOKENS, MODEL_WIDTH), 1.0, 6.0, ((0, 16), (2, 2))),
        "key_projection_weight": scatter_about(key_list[1], (MODEL_WIDTH, KEY_VALUE_HEADS * HEAD_SIZE), MODEL_WIDTH ** -0.5, 0.0625, ((0, 32),)),
        "value_projection_weight": scatter_about(key_list[2], (MODEL_WIDTH, KEY_VALUE_HEADS * HEAD_SIZE), MODEL_WIDTH ** -0.5, 0.0625, ((0, 32),)),
        "key_gain": jnp.clip(1.0 + 0.18 * jax.random.normal(key_list[3], (HEAD_SIZE,), jnp.float32), 0.1, 1.9),
        "queries": draw_queries(jax.random.fold_in(key_list[9], 71), 0),
        "out_grad": scatter_about(key_list[5], (DOCS, LEN, HQ * HEAD_SIZE), 1.0, 6.0, ((0, 16), (1, 2))),
        "image_ids": place_ends(jax.random.randint(key_list[6], (DOCS, IMAGE_SLOTS), 0, IMAGES_TOTAL), jax.random.fold_in(key_list[6], 1), 0, IMAGES_TOTAL - 1).astype(jnp.int32),
        "image_counts": place_ends(jax.random.randint(key_list[7], (DOCS,), 4, IMAGE_SLOTS + 1), jax.random.fold_in(key_list[7], 1), 4, IMAGE_SLOTS).astype(jnp.int32),
        "image_starts": place_ends(jax.random.randint(key_list[8], (DOCS, IMAGE_SLOTS), 0, LEN), jax.random.fold_in(key_list[8], 1), 0, LEN - 1).astype(jnp.int32),
    }


norm_epsilon = 1e-05

def key_norm(key_before_projection, key_gain):
    mean_square = lax.optimization_barrier(jnp.mean(key_before_projection * key_before_projection, axis=-1, keepdims=True))
    return key_before_projection * lax.rsqrt(mean_square + norm_epsilon) * key_gain

def visibility(row_sum_total, starts, image_count, image_tokens):
    key_slot = jnp.arange(starts.shape[0] * image_tokens, dtype=jnp.int32) // image_tokens
    slot_start = jnp.repeat(starts, image_tokens)
    position = jnp.arange(row_sum_total, dtype=jnp.int32)[:, None]
    return (key_slot[None, :] < image_count) & ((position >= slot_start[None, :]) | (key_slot[None, :] == 0))

def head_pass(query_head, grad_head, key_head, value_head, visible):
    score_scale = 1.0 / math.sqrt(query_head.shape[-1])
    scores = jnp.dot(query_head, key_head.T, preferred_element_type=jnp.float32) * score_scale
    scores = jnp.where(visible, scores, -1e+30)
    row_max = lax.optimization_barrier(jnp.max(scores, axis=-1, keepdims=True))
    weights = jnp.exp(scores - row_max)
    prob_rows = weights / lax.optimization_barrier(jnp.sum(weights, axis=-1, keepdims=True))
    probs_low = prob_rows.astype(jnp.bfloat16)
    attended = jnp.dot(probs_low, value_head, preferred_element_type=jnp.float32).astype(jnp.bfloat16)
    grad_probs = jnp.dot(grad_head, value_head.T, preferred_element_type=jnp.float32)
    row_delta = lax.optimization_barrier(jnp.sum(grad_head.astype(jnp.float32) * attended.astype(jnp.float32), axis=-1, keepdims=True))
    grad_scores = (prob_rows * (grad_probs - row_delta) * score_scale).astype(jnp.bfloat16)
    grad_query = jnp.dot(grad_scores, key_head, preferred_element_type=jnp.float32).astype(jnp.bfloat16)
    key_gradient = jnp.dot(grad_scores.T, query_head, preferred_element_type=jnp.float32)
    value_gradient = jnp.dot(probs_low.T, grad_head, preferred_element_type=jnp.float32)
    return (attended, grad_query, key_gradient, value_gradient)

def document_pass(query_rows, grad_rows, key_heads, value_heads, visible):
    row_sum_total = query_rows.shape[0]
    query_heads = query_rows.shape[1] // HEAD_SIZE
    kv_heads = key_heads.shape[0]
    group_size = query_heads // kv_heads
    query_split = query_rows.reshape(row_sum_total, query_heads, HEAD_SIZE).transpose(1, 0, 2)
    grad_split = grad_rows.reshape(row_sum_total, query_heads, HEAD_SIZE).transpose(1, 0, 2)

    def per_head(head_index):
        kv_index = head_index // group_size
        return head_pass(query_split[head_index], grad_split[head_index], key_heads[kv_index], value_heads[kv_index], visible)
    attended, grad_query, key_gradient, value_gradient = lax.map(per_head, jnp.arange(query_heads, dtype=jnp.int32))
    attended = attended.transpose(1, 0, 2).reshape(row_sum_total, query_heads * HEAD_SIZE)
    grad_query = grad_query.transpose(1, 0, 2).reshape(row_sum_total, query_heads * HEAD_SIZE)
    key_total = key_heads.shape[1]
    key_gradient = key_gradient.reshape(kv_heads, group_size, key_total, HEAD_SIZE).sum(axis=1)
    value_gradient = value_gradient.reshape(kv_heads, group_size, key_total, HEAD_SIZE).sum(axis=1)
    return (attended, grad_query, key_gradient, value_gradient)

def reference(vision, key_projection_weight, value_projection_weight, key_gain, queries, out_grad, image_ids, image_counts, image_starts):
    picture_rows = vision.reshape(IMAGES_TOTAL * IMAGE_TOKENS, MODEL_WIDTH)
    key_before_projection = jnp.dot(picture_rows, key_projection_weight, preferred_element_type=jnp.float32).reshape(IMAGES_TOTAL, IMAGE_TOKENS, KEY_VALUE_HEADS, HEAD_SIZE)
    value_before_projection = jnp.dot(picture_rows, value_projection_weight, preferred_element_type=jnp.float32).reshape(IMAGES_TOTAL, IMAGE_TOKENS, KEY_VALUE_HEADS, HEAD_SIZE)
    key_rows = key_norm(key_before_projection, key_gain).astype(jnp.bfloat16)
    value_rows = value_before_projection.astype(jnp.bfloat16)

    def per_doc(running, doc_inputs):
        query_rows, grad_rows, document_index, doc_count, doc_starts = doc_inputs
        slotted_keys = key_rows[document_index].reshape(IMAGE_SLOTS * IMAGE_TOKENS, KEY_VALUE_HEADS, HEAD_SIZE).transpose(1, 0, 2)
        slotted_values = value_rows[document_index].reshape(IMAGE_SLOTS * IMAGE_TOKENS, KEY_VALUE_HEADS, HEAD_SIZE).transpose(1, 0, 2)
        visible = visibility(LEN, doc_starts, doc_count, IMAGE_TOKENS)
        attended, grad_query, key_gradient, value_gradient = document_pass(query_rows, grad_rows, slotted_keys, slotted_values, visible)
        slot_gradients = jnp.stack((key_gradient, value_gradient), axis=1).reshape(KEY_VALUE_HEADS, 2, IMAGE_SLOTS, IMAGE_TOKENS, HEAD_SIZE)
        selector = (document_index[None, :] == jnp.arange(IMAGES_TOTAL, dtype=jnp.int32)[:, None]).astype(jnp.float32)
        image_part = jnp.einsum('es,hcstd->ethcd', selector, slot_gradients, precision=lax.Precision.HIGHEST)
        return (running + image_part, (attended, grad_query))
    zeroed_gradients = jnp.zeros((IMAGES_TOTAL, IMAGE_TOKENS, KEY_VALUE_HEADS, 2, HEAD_SIZE), jnp.float32)
    image_gradients, outputs = lax.scan(per_doc, zeroed_gradients, (queries, out_grad, image_ids, image_counts, image_starts))
    attended, grad_queries = outputs
    unused_out, norm_back = jax.vjp(lambda pre_norm: key_norm(pre_norm, key_gain), key_before_projection)
    key_backward_pass = norm_back(image_gradients[:, :, :, 0])[0]
    key_reduced_precision = key_backward_pass.astype(jnp.bfloat16).reshape(IMAGES_TOTAL * IMAGE_TOKENS, KEY_VALUE_HEADS * HEAD_SIZE)
    value_reduced_precision = image_gradients[:, :, :, 1].astype(jnp.bfloat16).reshape(IMAGES_TOTAL * IMAGE_TOKENS, KEY_VALUE_HEADS * HEAD_SIZE)
    contract = (((0,), (0,)), ((), ()))
    grad_wkey = lax.dot_general(picture_rows, key_reduced_precision, contract, preferred_element_type=jnp.float32)
    grad_wvalue = lax.dot_general(picture_rows, value_reduced_precision, contract, preferred_element_type=jnp.float32)
    return (attended, grad_queries, grad_wkey, grad_wvalue)
```

```python
import functools
import math

import jax
import jax.numpy as jnp
from jax import lax
from jax.experimental import pallas as pl
from jax.experimental.pallas import tpu as pltpu
from jax.sharding import PartitionSpec as P

KEY_VALUE_HEADS = 8
HEAD_SIZE = 128
TILE = 128

norm_epsilon = 1e-05
bf16 = jnp.bfloat16
f32 = jnp.float32
f16 = jnp.float16
SUM_SCALE = 16.0


def key_norm(key_before_projection, key_gain):
    mean_square = jnp.mean(key_before_projection * key_before_projection, axis=-1, keepdims=True)
    return key_before_projection * lax.rsqrt(mean_square + norm_epsilon) * key_gain


def after(a, *done):
    return lax.optimization_barrier((a, *done))[0]


def swap_core(a):
    n = lax.axis_size("dp")
    return lax.ppermute(a, "dp", [(i, i ^ 1) for i in range(n)])


def swap_x(a):
    n = lax.axis_size("dp")
    return lax.ppermute(a, "dp", [(i, i ^ 2) for i in range(n)])


def shift_chip(a, k, r=0):
    n = lax.axis_size("dp")
    return lax.ppermute(a, "dp", [(i, ((i + 4 * k) % n) ^ (2 * r)) for i in range(n)])


def swap_y(a):
    return lax.ppermute(a, "sp", [(0, 1), (1, 0)])


def gather_y(a):
    if lax.axis_size("sp") == 2:
        return [a, swap_y(a)]
    whole = lax.all_gather(a, "sp", axis=0, tiled=False)
    return [whole[i] for i in range(lax.axis_size("sp"))]


def exchange_y(blocks):
    if lax.axis_size("sp") == 2:
        return [blocks[0], swap_y(blocks[1])]
    got = lax.all_to_all(jnp.stack(blocks), "sp", split_axis=0, concat_axis=0, tiled=True)
    return [got[i] for i in range(lax.axis_size("sp"))]


def split_y(a, axis):
    size = lax.axis_size("sp")
    parts = jnp.split(a, size, axis=axis)
    if size == 2:
        s = lax.axis_index("sp")
        half = a.shape[axis] // 2
        return [lax.dynamic_slice_in_dim(a, (s ^ r) * half, half, axis) for r in range(2)]
    return parts


def join_y(parts, axis):
    if lax.axis_size("sp") == 2:
        s = lax.axis_index("sp")
        return jnp.where(
            s == 0,
            jnp.concatenate(parts, axis=axis),
            jnp.concatenate(parts[::-1], axis=axis),
        )
    return jnp.concatenate(parts, axis=axis)


def turns(total):
    return [*range(2, total), 1, 0]


def reduce_chips(keep, send, total, kind=bf16):
    low = []
    for j in turns(total):
        other = swap_x(send[j])
        if j == 0:
            return [keep[0]], [*low, other]
        low.append(shift_chip((keep[j] + other.astype(f32)).astype(kind), -j))


def gather_chips(block, total):
    column = [None] * total
    column[0] = block
    up, down = block, block
    for step in range(1, total // 2 + 1):
        up = shift_chip(up, 1)
        column[step] = up
        if step < total - step:
            down = shift_chip(down, -1)
            column[total - step] = down
    return [b for block in column for b in (block, swap_x(block))]


def attention_kernel(group, scale, chunk, blocks, parts, images, pos_ref, start_ref, base_ref, *refs):
    q_ref, g_ref = refs[:2]
    kv_refs = refs[2 : 2 + blocks]
    att_ref, dq_ref = refs[2 + blocks : 4 + blocks]
    grad_refs = refs[4 + blocks : -12]
    qs, gs, gt, kv, kc, vc, kct, vct, weights, tops, turned, acc = refs[-12:]
    size = HEAD_SIZE
    slots = start_ref.shape[1]
    tokens = kv.shape[0] // images
    span = chunk * tokens
    doc = pl.program_id(1)
    rows = group * TILE

    @pl.when(doc == 0)
    def _():
        acc[...] = jnp.zeros_like(acc)
        for part in range(parts):

            @pl.when(pl.program_id(0) * parts // pl.num_programs(0) == part)
            def _():
                at = 0
                for ref in kv_refs[part::parts]:
                    kv[at : at + ref.shape[0], :] = ref[...]
                    at += ref.shape[0]

    for i in range(slots):
        row = pl.ds(pl.multiple_of(pos_ref[doc, i] * tokens, tokens), tokens)
        here = slice(i * tokens, (i + 1) * tokens)
        inside = slice(i % chunk * tokens, (i % chunk + 1) * tokens)
        k, v = kv[row, :size], kv[row, size:]
        kc[here, :] = k
        vc[here, :] = v
        kct[i // chunk, :, inside] = k.T
        vct[i // chunk, :, inside] = v.T

    def acc_rows(i):
        return pl.ds(pl.multiple_of(pos_ref[doc, i] * tokens, tokens), tokens)

    def tile_step(tile, carry):
        base = base_ref[tile]
        here = pl.ds(pl.multiple_of(tile * TILE, TILE), TILE)
        for h in range(group):
            qs[h * TILE : (h + 1) * TILE, :] = q_ref[here, h * size : (h + 1) * size]
            gs[h * TILE : (h + 1) * TILE, :] = g_ref[here, h * size : (h + 1) * size]
        gt[...] = gs[...].T
        n = jnp.int32(0)
        for i in range(slots):
            n = n + (start_ref[doc, i] < base + TILE).astype(jnp.int32)
        position = base + lax.broadcasted_iota(jnp.int32, (1, rows), 1) % TILE

        def run(chunks):
            top = jnp.full((1, rows), -1e30, f32)
            total = jnp.zeros((1, rows), f32)
            for j in range(chunks):
                s = lax.dot_general(
                    kc[j * span : (j + 1) * span, :],
                    qs[...],
                    (((1,), (1,)), ((), ())),
                    preferred_element_type=f32,
                )
                parts = []
                for i in range(chunk):
                    hidden = jnp.where(position >= start_ref[doc, chunk * j + i], 0.0, -1e30)
                    part = s[i * tokens : (i + 1) * tokens] * (scale * math.log2(math.e))
                    parts.append(part + hidden)
                s = jnp.concatenate(parts, 0)
                now = jnp.maximum(top, jnp.max(s, axis=0, keepdims=True))
                e = jnp.exp2(s - now)
                weights[j] = e
                tops[j] = now
                total = total * jnp.exp2(top - now) + jnp.sum(e, axis=0, keepdims=True)
                top = now
            inverse = 1.0 / total
            turned[...] = jnp.zeros_like(turned)
            for j in range(chunks):
                low = (weights[j] * (jnp.exp2(tops[j] - top) * inverse)).astype(bf16)
                turned[...] += jnp.dot(vct[j], low, preferred_element_type=f32)
                dv = jnp.dot(low, gs[...], preferred_element_type=f32)
                for i in range(chunk):
                    acc[acc_rows(chunk * j + i), size:] += dv[i * tokens : (i + 1) * tokens]
            att = turned[...].astype(bf16)
            for h in range(group):
                att_ref[here, h * size : (h + 1) * size] = att[:, h * TILE : (h + 1) * TILE].T
            delta = jnp.sum(gt[...].astype(f32) * att.astype(f32), axis=0, keepdims=True)
            turned[...] = jnp.zeros_like(turned)
            for j in range(chunks):
                dp = lax.dot_general(
                    vc[j * span : (j + 1) * span, :],
                    gs[...],
                    (((1,), (1,)), ((), ())),
                    preferred_element_type=f32,
                )
                p = weights[j] * (jnp.exp2(tops[j] - top) * (inverse * scale))
                ds = (p * (dp - delta)).astype(bf16)
                turned[...] += jnp.dot(kct[j], ds, preferred_element_type=f32)
                dk = jnp.dot(ds, qs[...], preferred_element_type=f32)
                for i in range(chunk):
                    acc[acc_rows(chunk * j + i), :size] += dk[i * tokens : (i + 1) * tokens]
            dq = turned[...].astype(bf16)
            for h in range(group):
                dq_ref[here, h * size : (h + 1) * size] = dq[:, h * TILE : (h + 1) * TILE].T

        used = (n + chunk - 1) // chunk
        for chunks in range(1, slots // chunk + 1):
            pl.when(used == chunks)(functools.partial(run, chunks))
        return carry

    lax.fori_loop(0, q_ref.shape[0] // TILE, tile_step, 0)

    @pl.when(doc == pl.num_programs(1) - 1)
    def _():
        at = 0
        for ref in grad_refs:
            ref[...] = acc[at : at + ref.shape[0], :].astype(ref.dtype)
            at += ref.shape[0]


def attention(both, kv_blocks, parts, pos, starts, bases):
    docs, slots = starts.shape
    length = both.shape[0] // docs
    kv_rows = sum(b.shape[0] for b in kv_blocks[::parts])
    kv_cols = kv_blocks[0].shape[1] * parts
    heads = kv_cols // (2 * HEAD_SIZE)
    width = both.shape[1] // 2
    span = width // heads
    group = span // HEAD_SIZE
    images = lax.axis_size("dp")
    tokens = kv_rows // images
    chunk = next(c for c in (4, 2, 1) if slots % c == 0)
    rows = group * TILE
    q_spec = pl.BlockSpec((length, span), lambda h, d, *_: (d, h))
    g_spec = pl.BlockSpec((length, span), lambda h, d, *_: (d, heads + h))
    each = heads // parts
    kv_specs = [
        pl.BlockSpec(
            (b.shape[0], 2 * HEAD_SIZE),
            lambda h, d, *_, part=i % parts: (0, jnp.clip(h - part * each, 0, each - 1)),
        )
        for i, b in enumerate(kv_blocks)
    ]
    count = lax.axis_size("dp") // 2
    grad_rows = kv_rows // count
    grad_spec = pl.BlockSpec((grad_rows, 2 * HEAD_SIZE), lambda h, d, *_: (0, h))
    grad_shapes = [
        jax.ShapeDtypeStruct((grad_rows, kv_cols), f32 if i < count // 2 else bf16)
        for i in range(count)
    ]
    grid_spec = pltpu.PrefetchScalarGridSpec(
        num_scalar_prefetch=3,
        grid=(heads, docs),
        in_specs=[q_spec, g_spec, *kv_specs],
        out_specs=[q_spec, q_spec] + [grad_spec] * count,
        scratch_shapes=[
            pltpu.VMEM((rows, HEAD_SIZE), bf16),
            pltpu.VMEM((rows, HEAD_SIZE), bf16),
            pltpu.VMEM((HEAD_SIZE, rows), bf16),
            pltpu.VMEM((kv_rows, 2 * HEAD_SIZE), bf16),
            pltpu.VMEM((slots * tokens, HEAD_SIZE), bf16),
            pltpu.VMEM((slots * tokens, HEAD_SIZE), bf16),
            pltpu.VMEM((slots // chunk, HEAD_SIZE, chunk * tokens), bf16),
            pltpu.VMEM((slots // chunk, HEAD_SIZE, chunk * tokens), bf16),
            pltpu.VMEM((slots // chunk, chunk * tokens, rows), f32),
            pltpu.VMEM((slots // chunk, 1, rows), f32),
            pltpu.VMEM((HEAD_SIZE, rows), f32),
            pltpu.VMEM((kv_rows, 2 * HEAD_SIZE), f32),
        ],
    )
    out_shape = jax.ShapeDtypeStruct((docs * length, width), bf16)
    return pl.pallas_call(
        functools.partial(
            attention_kernel, group, 1.0 / math.sqrt(HEAD_SIZE), chunk, len(kv_blocks), parts, images
        ),
        grid_spec=grid_spec,
        out_shape=[out_shape, out_shape, *grad_shapes],
        compiler_params=pltpu.CompilerParams(
            vmem_limit_bytes=(12 << 20) + 16 * kv_rows * 2 * HEAD_SIZE + 24 * length * span
        ),
        cost_estimate=pl.CostEstimate(
            flops=12 * docs * length * width * slots * tokens,
            bytes_accessed=8 * docs * length * width + 5 * kv_rows * kv_cols,
            transcendentals=docs * length * width // HEAD_SIZE * slots * tokens,
        ),
        name="attention",
    )(pos, starts, bases, both, both, *kv_blocks)


def whole_call(kernel, out_shape, args, flops, name, scalar=None):
    vmem = pl.BlockSpec(memory_space=pltpu.VMEM)
    smem = pl.BlockSpec(memory_space=pltpu.SMEM)
    scalars = [] if scalar is None else [scalar.reshape(-1).astype(jnp.int32)]
    moved = sum(a.size * a.dtype.itemsize for a in (*args, *out_shape))
    return pl.pallas_call(
        kernel,
        out_shape=out_shape,
        in_specs=[smem] * len(scalars) + [vmem] * len(args),
        out_specs=[vmem] * len(out_shape),
        compiler_params=pltpu.CompilerParams(vmem_limit_bytes=16 * 1024 * 1024),
        cost_estimate=pl.CostEstimate(flops=flops, bytes_accessed=moved, transcendentals=0),
        name=name,
    )(*scalars, *args)


def in_order(core, own, other):
    return jnp.where(core == 0, own, other), jnp.where(core == 0, other, own)


def project(seen, weights, core):
    count = len(weights)
    tokens, features = seen[0][0].shape
    width = weights[0][0].shape[1] // 2

    def kernel(core_ref, *refs):
        outs = refs[4 * count :]
        totals = [None, None]
        for y in range(count):
            own, other = refs[2 * count + 2 * y : 2 * count + 2 * y + 2]
            w = jnp.concatenate(in_order(core_ref[0], own[...], other[...]), 0)
            for r in range(2):
                term = jnp.dot(refs[r * count + y][...], w, preferred_element_type=f32)
                totals[r] = term if totals[r] is None else totals[r] + term
        for total, out in zip(totals, outs, strict=True):
            for h in range(width // HEAD_SIZE):
                for kind in range(2):
                    c = (2 * h + kind) * HEAD_SIZE
                    t = total[:, kind * width + h * HEAD_SIZE :][:, :HEAD_SIZE]
                    out[:, c : c + HEAD_SIZE] = (t * SUM_SCALE).astype(out.dtype)

    shape = (tokens, 2 * width)
    shapes = [jax.ShapeDtypeStruct(shape, f32), jax.ShapeDtypeStruct(shape, f32)]
    flops = 8 * tokens * width * features * count
    args = [*seen[0], *seen[1], *(w for pair in weights for w in pair)]
    return whole_call(kernel, shapes, args, flops, "project", core)


def total_of(refs):
    total = refs[0][...]
    for ref in refs[1:]:
        total = total + ref[...].astype(f32)
    return total


def norm_forward(high, low, gain, core, halves):
    terms = [*high, *low]

    def kernel(core_ref, *refs):
        gain_ref, pre_ref = refs[len(terms) : len(terms) + 2]
        outs = refs[len(terms) + 2 :]
        total = total_of(refs[: len(terms)]) * (1.0 / SUM_SCALE)
        pre_ref[...] = total
        blocks = []
        for c in range(0, total.shape[1], 2 * HEAD_SIZE):
            blocks.append(key_norm(total[:, c : c + HEAD_SIZE], gain_ref[...]).astype(bf16))
            blocks.append(total[:, c + HEAD_SIZE : c + 2 * HEAD_SIZE].astype(bf16))
        low = jnp.concatenate(blocks, 1)
        if halves == 2:
            half = low.shape[1] // 2
            outs[0][...], outs[1][...] = in_order(core_ref[0], low[:, :half], low[:, half:])
        else:
            outs[0][...] = low

    rows, cols = terms[0].shape
    shapes = [jax.ShapeDtypeStruct((rows, cols), f32)]
    shapes += [jax.ShapeDtypeStruct((rows, cols // halves), bf16)] * halves
    outs = whole_call(kernel, shapes, [*terms, gain], 8 * rows * cols, "norm_forward", core)
    return outs[0], outs[1:]


def sum_terms(parts):
    counts = [len(high) + len(low) for high, low in parts]
    terms = [t for high, low in parts for t in (*high, *low)]

    def kernel(*refs):
        mine_ref, theirs_ref = refs[len(terms) :]
        half, cols = mine_ref.shape[0], refs[0].shape[1]
        for p, count in enumerate(counts):
            total = total_of(refs[sum(counts[:p]) : sum(counts[:p]) + count])
            here = slice(p * cols, (p + 1) * cols)
            mine_ref[:, here] = total[:half]
            theirs_ref[:, here] = total[half:]

    rows, cols = terms[0].shape
    shapes = [jax.ShapeDtypeStruct((rows // 2, len(parts) * cols), f32)] * 2
    return whole_call(kernel, shapes, terms, rows * cols * len(terms), "sum_terms")


def norm_backward(parts, high, low, pre, gain, core):
    terms = [*parts, *high, *low]

    def kernel(core_ref, *refs):
        pre_ref, gain_ref, out_ref = refs[len(terms) :]
        if parts:
            total = jnp.concatenate(in_order(core_ref[0], refs[0][...], refs[1][...]), 1)
        else:
            total = total_of(refs[: len(terms)])
        for c in range(0, total.shape[1], 2 * HEAD_SIZE):
            k = slice(c, c + HEAD_SIZE)
            x = pre_ref[:, k]
            inverse = lax.rsqrt(jnp.mean(x * x, axis=-1, keepdims=True) + norm_epsilon)
            up = total[:, k] * gain_ref[...]
            mean = jnp.mean(up * x, axis=-1, keepdims=True)
            out_ref[:, k] = (inverse * (up - x * (inverse * inverse * mean))).astype(bf16)
            v = slice(c + HEAD_SIZE, c + 2 * HEAD_SIZE)
            out_ref[:, v] = total[:, v].astype(bf16)

    shapes = [jax.ShapeDtypeStruct(pre.shape, bf16)]
    args = [*terms, pre, gain]
    return whole_call(kernel, shapes, args, 12 * pre.size, "norm_backward", core)[0]


def place_columns(pieces, width, places):
    arrays = list({id(a): a for a, _, _ in pieces}.values())
    index = {id(a): i for i, a in enumerate(arrays)}
    rows = min(a.shape[0] for a in arrays)

    def kernel(place_ref, *refs):
        for i, (a, row, col) in enumerate(pieces):
            to = pl.ds(pl.multiple_of(place_ref[i] * width, width), width)
            refs[-1][:, to] = refs[index[id(a)]][row : row + rows, col : col + width]

    shapes = [jax.ShapeDtypeStruct((rows, len(pieces) * width), arrays[0].dtype)]
    return whole_call(kernel, shapes, arrays, 0, "place_columns", places)[0]


def weight_gradient(seen, back, core):
    count, parts = len(seen), len(back)

    def kernel(core_ref, *refs):
        mine_ref, theirs_ref = refs[-2:]
        half, cols = mine_ref.shape[0], refs[count].shape[1]
        for p in range(parts):
            total = None
            for a, b in zip(refs[:count], refs[count * (p + 1) : count * (p + 2)], strict=True):
                term = lax.dot_general(
                    a[...], b[...], (((0,), (0,)), ((), ())), preferred_element_type=f32
                )
                total = term if total is None else total + term
            here = slice(p * cols, (p + 1) * cols)
            mine, theirs = in_order(core_ref[0], total[:half], total[half:])
            mine_ref[:, here] = mine
            theirs_ref[:, here] = theirs

    half, cols = seen[0].shape[1] // 2, back[0][0].shape[1] * parts
    shapes = [jax.ShapeDtypeStruct((half, cols), f32)] * 2
    flops = 4 * half * cols * count * seen[0].shape[0]
    args = [*seen, *(b for part in back for b in part)]
    return whole_call(kernel, shapes, args, flops, "weight_gradient", core)


def split_heads(parts, index):
    ys = len(parts[0])
    rows, cols = parts[0][0][0].shape
    args = [t for part in parts for block in part for t in block]

    def kernel(index_ref, *refs):
        outs = refs[-2:]

        def place(order):
            it = iter(refs)
            for p, part in enumerate(parts):
                for block, to in zip(part, order, strict=True):
                    terms = [next(it)[...].astype(f32) for _ in block]
                    total = sum(terms[1:], terms[0])
                    for c in range(0, cols, HEAD_SIZE):
                        h = (to * len(parts) + p) * (cols // 2)
                        h += c // (2 * HEAD_SIZE) * HEAD_SIZE
                        out = outs[c // HEAD_SIZE % 2]
                        out[:, h : h + HEAD_SIZE] = total[:, c : c + HEAD_SIZE]

        if ys == 2:
            for i in range(2):
                pl.when(index_ref[0] == i)(functools.partial(place, (i, 1 - i)))
        else:
            place(range(ys))

    shapes = [jax.ShapeDtypeStruct((rows, ys * len(parts) * cols // 2), f32)] * 2
    return whole_call(kernel, shapes, args, 0, "split_heads", index)


def shards(
    vision,
    key_projection_weight,
    value_projection_weight,
    key_gain,
    queries,
    out_grad,
    image_ids,
    image_counts,
    image_starts,
):
    dp = lax.axis_size("dp")
    sp = lax.axis_size("sp")
    levels = dp // 4
    d = lax.axis_index("dp")
    s = lax.axis_index("sp")
    z, x, core = d // 4, (d // 2) % 2, d % 2
    tokens = vision.shape[0] * vision.shape[1]
    own_vision = vision.reshape(tokens, vision.shape[2])
    heads = KEY_VALUE_HEADS // sp
    rows_here = key_projection_weight.shape[0]

    keys = split_y(key_projection_weight, 1)
    values = split_y(value_projection_weight, 1)
    weights = exchange_y(
        [jnp.concatenate(pair, 1) for pair in zip(keys, values, strict=True)]
    )
    weights = [(w, swap_core(w)) for w in weights]

    order = [*range(1, levels), 0]
    pieces = {}
    for j in order:
        for r in range(2):
            chip = (z + j) % levels * 2 + (x ^ r)
            piece = lax.dynamic_slice_in_dim(own_vision, chip * 2 * rows_here, 2 * rows_here, 1)
            if j > 1:
                piece = after(piece, pieces[j - 1, r])
            pieces[j, r] = piece if j == 0 and r == 0 else shift_chip(piece, j, r)
    seen = [None] * (2 * levels)
    moved = [weights[-1][0]]
    terms = [None] * levels
    for n, j in enumerate(order):
        for r in range(2):
            piece = pieces[j, r]
            if len(moved) > 1:
                piece = after(piece, moved[-2])
            seen[2 * j + r] = gather_y(piece)
            moved.append(seen[2 * j + r][-1])
        terms[j] = project(seen[2 * j : 2 * j + 2], weights, core)

    halves = 2 if heads % 2 == 0 else 1
    queries, out_grad = after(queries, moved[-1]), after(out_grad, moved[-1])
    queries, out_grad = split_y(queries[0], 1), split_y(out_grad[0], 1)
    both = exchange_y([jnp.concatenate(pair, 1) for pair in zip(queries, out_grad, strict=True)])
    both = jnp.concatenate(both, 0)
    length = both.shape[0]
    if halves == 2:
        half = both.shape[1] // 4
        cuts = [
            jnp.concatenate(
                [
                    lax.dynamic_slice_in_dim(both, (2 * kind + (core ^ c)) * half, half, 1)
                    for kind in range(2)
                ],
                1,
            )
            for c in range(2)
        ]
        both = jnp.concatenate((cuts[0], swap_core(cuts[1])), 0)

    gain = key_gain.reshape(1, HEAD_SIZE)
    high, low = reduce_chips([t[0] for t in terms], [t[1].astype(f16) for t in terms], levels, f16)
    total = sum([a.astype(f32) for a in low], high[0])
    pre, pairs = norm_forward([total], [], gain, core, halves)
    block = pairs[0]
    if halves == 2:
        block = jnp.concatenate((block, swap_core(pairs[1])), 0)
    if halves == 2:
        column = gather_chips(block, levels)
        kv_blocks = column[::2] + column[1::2]
    else:
        column = gather_chips(block, levels)
        kv_blocks = [*column, swap_core(jnp.concatenate(column, 0))]

    ids = image_ids[0].astype(jnp.int32)
    slot = jnp.arange(ids.shape[0], dtype=jnp.int32)
    first = jnp.where(slot == 0, -1, image_starts[0])
    first = jnp.where(slot < image_counts[0], first, 1 << 30)
    before = (first[None, :] < first[:, None]) | (
        (first[None, :] == first[:, None]) & (slot[None, :] < slot[:, None])
    )
    rank = jnp.sum(before.astype(jnp.int32), axis=1)
    turn = (rank[None, :] == slot[:, None]).astype(jnp.int32)
    table = jnp.sum(turn[None] * jnp.stack((ids, first))[:, None, :], axis=2)[None]
    if halves == 2:
        table = jnp.concatenate((table, swap_core(table)), 0)
    ids, first = table[:, 0], table[:, 1]
    level, far, mate = (z - ids // 4) % levels, x ^ (ids // 2 % 2), core ^ (ids % 2)
    if halves == 2:
        place = (far * levels + level) * 2 + mate
    else:
        place = (mate * levels + level) * 2 + far
    local = length // sp
    at = jnp.arange(length // TILE, dtype=jnp.int32) * TILE
    if sp == 2:
        at = (at + s * local) % length
    attended, grad_query, *blocks = attention(both, kv_blocks, 1, place, first, at)

    width = attended.shape[1]
    sources = [(attended, 0), (grad_query, 0)]
    if halves == 2:
        theirs = swap_core(jnp.concatenate((attended[length:], grad_query[length:]), 1))
        sources += [(theirs, 0), (theirs, width)]
    got = exchange_y(
        [
            jnp.concatenate(
                [a[y * local : (y + 1) * local, c : c + width] for a, c in sources], 1
            )
            for y in range(sp)
        ]
    )
    pieces = [[], []]
    for y in range(sp):
        for i, (a, c) in enumerate(sources):
            own = y == 0 and sp == 2
            pieces[i % 2].append((a, 0, c) if own else (got[y], 0, i * width))
    ys = [s ^ y if sp == 2 else y for y in range(sp)]
    places = jnp.stack([y * halves + (core ^ c) * (halves - 1) for y in ys for c in range(halves)])
    attended_out, query_out = [place_columns(p, width, places) for p in pieces]

    keeps, sends = blocks[:levels], blocks[levels:]
    if halves == 1:
        sums = [k + swap_core(a).astype(f32) for k, a in zip(keeps, sends, strict=True)]
        keeps = [a[:tokens] for a in sums]
        sends = [a[tokens:].astype(bf16) for a in sums]
        high, low = reduce_chips(keeps, sends, levels)
        back = norm_backward([], high, low, pre, gain, core)
    else:
        totals = [reduce_chips(keeps, sends, levels)]
        mine, theirs = sum_terms(totals)
        back = norm_backward((mine, swap_core(theirs)), [], [], pre, gain, core)
    back = after(back, *got)
    back = [gather_chips(b, levels) for b in jnp.split(back, halves, axis=1)]

    for p in range(len(back) - 1):
        back[p][0] = after(back[p][0], back[p + 1][1], *back[p + 1][2::2])
    grads = []
    for part in back:
        if grads:
            part = [after(part[0], *(a for y in grads[-1] for a in y)), *part[1:]]
        sent = []
        for y in reversed(range(sp)):
            mine, theirs = weight_gradient([block[y] for block in seen], [part], core)
            other = swap_core(theirs)
            if y > 0 or sp > 2:
                sent.append((mine + other).astype(bf16))
        if sp == 2:
            grads.append([(mine, other), (swap_y(sent[0]),)])
        else:
            grads.append([(a,) for a in exchange_y(sent[::-1])])
    grad_key, grad_value = split_heads(grads, s)
    return attended_out[None], query_out[None], grad_key, grad_value


def solution(mesh):
    return jax.shard_map(
        shards,
        mesh=mesh,
        in_specs=(
            P("dp", None, "sp"),
            P(("sp", "dp"), None),
            P(("sp", "dp"), None),
            P(),
            P("dp", "sp", None),
            P("dp", "sp", None),
            P("dp", None),
            P("dp"),
            P("dp", None),
        ),
        out_specs=(
            P("dp", "sp", None),
            P("dp", "sp", None),
            P(("sp", "dp"), None),
            P(("sp", "dp"), None),
        ),
        check_vma=False,
    )
```

```python
import functools
import math

import jax
import jax.numpy as jnp
from jax import lax
from jax.experimental import pallas as pl
from jax.experimental.pallas import tpu as pltpu
from jax.sharding import PartitionSpec as P

KEY_VALUE_HEADS = 8
HEAD_SIZE = 128
TILE = 128
CHUNK = 8

norm_epsilon = 1e-05
bf16 = jnp.bfloat16
f32 = jnp.float32
f16 = jnp.float16
SUM_SCALE = 16.0


def key_norm(key_before_projection, key_gain):
    mean_square = jnp.mean(key_before_projection * key_before_projection, axis=-1, keepdims=True)
    return key_before_projection * lax.rsqrt(mean_square + norm_epsilon) * key_gain


def after(a, *done):
    return lax.optimization_barrier((a, *done))[0]


def swap_core(a):
    n = lax.axis_size("dp")
    return lax.ppermute(a, "dp", [(i, i ^ 1) for i in range(n)])


def swap_x(a):
    n = lax.axis_size("dp")
    return lax.ppermute(a, "dp", [(i, i ^ 2) for i in range(n)])


def shift_chip(a, k, r=0):
    n = lax.axis_size("dp")
    return lax.ppermute(a, "dp", [(i, ((i + 4 * k) % n) ^ (2 * r)) for i in range(n)])


def swap_y(a):
    return lax.ppermute(a, "sp", [(0, 1), (1, 0)])


def gather_y(a):
    if lax.axis_size("sp") == 2:
        return [a, swap_y(a)]
    whole = lax.all_gather(a, "sp", axis=0, tiled=False)
    return [whole[i] for i in range(lax.axis_size("sp"))]


def exchange_y(blocks):
    if lax.axis_size("sp") == 2:
        return [blocks[0], swap_y(blocks[1])]
    got = lax.all_to_all(jnp.stack(blocks), "sp", split_axis=0, concat_axis=0, tiled=True)
    return [got[i] for i in range(lax.axis_size("sp"))]


def split_y(a, axis):
    size = lax.axis_size("sp")
    parts = jnp.split(a, size, axis=axis)
    if size == 2:
        s = lax.axis_index("sp")
        half = a.shape[axis] // 2
        return [lax.dynamic_slice_in_dim(a, (s ^ r) * half, half, axis) for r in range(2)]
    return parts


def join_y(parts, axis):
    if lax.axis_size("sp") == 2:
        s = lax.axis_index("sp")
        return jnp.where(
            s == 0,
            jnp.concatenate(parts, axis=axis),
            jnp.concatenate(parts[::-1], axis=axis),
        )
    return jnp.concatenate(parts, axis=axis)


def turns(total):
    return [*range(2, total), 1, 0]


def reduce_chips(keep, send, total, kind=bf16):
    low = []
    for j in turns(total):
        other = swap_x(send[j])
        if j == 0:
            return [keep[0]], [*low, other]
        low.append(shift_chip((keep[j] + other.astype(f32)).astype(kind), -j))


def gather_chips(block, total):
    column = [None] * total
    column[0] = block
    up, down = block, block
    for step in range(1, total // 2 + 1):
        up = shift_chip(up, 1)
        column[step] = up
        if step < total - step:
            down = shift_chip(down, -1)
            column[total - step] = down
    return [b for block in column for b in (block, swap_x(block))]


def attention_kernel(group, scale, chunk, blocks, parts, images, pos_ref, start_ref, base_ref, *refs):
    q_ref, g_ref = refs[:2]
    kv_refs = refs[2 : 2 + blocks]
    att_ref, dq_ref = refs[2 + blocks : 4 + blocks]
    grad_refs = refs[4 + blocks : -12]
    qs, gs, gt, kv, kc, vc, kct, vct, weights, tops, turned, acc = refs[-12:]
    size = HEAD_SIZE
    slots = start_ref.shape[1]
    tokens = kv.shape[0] // images
    unit = 2 if slots % 2 == 0 else 1
    doc = pl.program_id(1)
    rows = group * TILE

    @pl.when(doc == 0)
    def _():
        acc[...] = jnp.zeros_like(acc)
        for part in range(parts):

            @pl.when(pl.program_id(0) * parts // pl.num_programs(0) == part)
            def _():
                at = 0
                for ref in kv_refs[part::parts]:
                    kv[at : at + ref.shape[0], :] = ref[...]
                    at += ref.shape[0]

    for i in range(slots):
        row = pl.ds(pl.multiple_of(pos_ref[doc, i] * tokens, tokens), tokens)
        here = slice(i * tokens, (i + 1) * tokens)
        k, v = kv[row, :size], kv[row, size:]
        kc[here, :] = k
        vc[here, :] = v
        kct[:, here] = k.T
        vct[:, here] = v.T

    def acc_rows(i):
        return pl.ds(pl.multiple_of(pos_ref[doc, i] * tokens, tokens), tokens)

    def tile_step(tile, carry):
        base = base_ref[tile]
        here = pl.ds(pl.multiple_of(tile * TILE, TILE), TILE)
        for h in range(group):
            qs[h * TILE : (h + 1) * TILE, :] = q_ref[here, h * size : (h + 1) * size]
            gs[h * TILE : (h + 1) * TILE, :] = g_ref[here, h * size : (h + 1) * size]
        gt[...] = gs[...].T
        n = jnp.int32(0)
        for i in range(slots):
            n = n + (start_ref[doc, i] < base + TILE).astype(jnp.int32)
        position = base + lax.broadcasted_iota(jnp.int32, (1, rows), 1) % TILE

        def run(most):
            cuts = [(i, min(i + chunk, most)) for i in range(0, most, chunk)]
            top = jnp.full((1, rows), -1e30, f32)
            total = jnp.zeros((1, rows), f32)
            for j, (lo, hi) in enumerate(cuts):
                s = lax.dot_general(
                    kc[lo * tokens : hi * tokens, :],
                    qs[...],
                    (((1,), (1,)), ((), ())),
                    preferred_element_type=f32,
                )
                parts = []
                for i in range(lo, hi):
                    hidden = jnp.where(position >= start_ref[doc, i], 0.0, -1e30)
                    part = s[(i - lo) * tokens :][:tokens] * (scale * math.log2(math.e))
                    parts.append(part + hidden)
                s = jnp.concatenate(parts, 0)
                now = jnp.maximum(top, jnp.max(s, axis=0, keepdims=True))
                e = jnp.exp2(s - now)
                weights[lo * tokens : hi * tokens, :] = e
                tops[j] = now
                total = total * jnp.exp2(top - now) + jnp.sum(e, axis=0, keepdims=True)
                top = now
            inverse = 1.0 / total
            turned[...] = jnp.zeros_like(turned)
            for j, (lo, hi) in enumerate(cuts):
                low = (weights[lo * tokens : hi * tokens, :] * (jnp.exp2(tops[j] - top) * inverse)).astype(bf16)
                turned[...] += jnp.dot(vct[:, lo * tokens : hi * tokens], low, preferred_element_type=f32)
                dv = jnp.dot(low, gs[...], preferred_element_type=f32)
                for i in range(lo, hi):
                    acc[acc_rows(i), size:] += dv[(i - lo) * tokens :][:tokens]
            att = turned[...].astype(bf16)
            for h in range(group):
                att_ref[here, h * size : (h + 1) * size] = att[:, h * TILE : (h + 1) * TILE].T
            delta = jnp.sum(gt[...].astype(f32) * att.astype(f32), axis=0, keepdims=True)
            turned[...] = jnp.zeros_like(turned)
            for j, (lo, hi) in enumerate(cuts):
                dp = lax.dot_general(
                    vc[lo * tokens : hi * tokens, :],
                    gs[...],
                    (((1,), (1,)), ((), ())),
                    preferred_element_type=f32,
                )
                p = weights[lo * tokens : hi * tokens, :] * (jnp.exp2(tops[j] - top) * (inverse * scale))
                ds = (p * (dp - delta)).astype(bf16)
                turned[...] += jnp.dot(kct[:, lo * tokens : hi * tokens], ds, preferred_element_type=f32)
                dk = jnp.dot(ds, qs[...], preferred_element_type=f32)
                for i in range(lo, hi):
                    acc[acc_rows(i), :size] += dk[(i - lo) * tokens :][:tokens]
            dq = turned[...].astype(bf16)
            for h in range(group):
                dq_ref[here, h * size : (h + 1) * size] = dq[:, h * TILE : (h + 1) * TILE].T

        used = (n + unit - 1) // unit
        for count in range(1, slots // unit + 1):
            pl.when(used == count)(functools.partial(run, count * unit))
        return carry

    lax.fori_loop(0, q_ref.shape[0] // TILE, tile_step, 0)

    @pl.when(doc == pl.num_programs(1) - 1)
    def _():
        at = 0
        for ref in grad_refs:
            ref[...] = acc[at : at + ref.shape[0], :].astype(ref.dtype)
            at += ref.shape[0]


def attention(both, kv_blocks, parts, pos, starts, bases):
    docs, slots = starts.shape
    length = both.shape[0] // docs
    kv_rows = sum(b.shape[0] for b in kv_blocks[::parts])
    kv_cols = kv_blocks[0].shape[1] * parts
    heads = kv_cols // (2 * HEAD_SIZE)
    width = both.shape[1] // 2
    span = width // heads
    group = span // HEAD_SIZE
    images = lax.axis_size("dp")
    tokens = kv_rows // images
    chunk = CHUNK
    rows = group * TILE
    q_spec = pl.BlockSpec((length, span), lambda h, d, *_: (d, h))
    g_spec = pl.BlockSpec((length, span), lambda h, d, *_: (d, heads + h))
    each = heads // parts
    kv_specs = [
        pl.BlockSpec(
            (b.shape[0], 2 * HEAD_SIZE),
            lambda h, d, *_, part=i % parts: (0, jnp.clip(h - part * each, 0, each - 1)),
        )
        for i, b in enumerate(kv_blocks)
    ]
    count = lax.axis_size("dp") // 2
    grad_rows = kv_rows // count
    grad_spec = pl.BlockSpec((grad_rows, 2 * HEAD_SIZE), lambda h, d, *_: (0, h))
    grad_shapes = [
        jax.ShapeDtypeStruct((grad_rows, kv_cols), f32 if i < count // 2 else bf16)
        for i in range(count)
    ]
    grid_spec = pltpu.PrefetchScalarGridSpec(
        num_scalar_prefetch=3,
        grid=(heads, docs),
        in_specs=[q_spec, g_spec, *kv_specs],
        out_specs=[q_spec, q_spec] + [grad_spec] * count,
        scratch_shapes=[
            pltpu.VMEM((rows, HEAD_SIZE), bf16),
            pltpu.VMEM((rows, HEAD_SIZE), bf16),
            pltpu.VMEM((HEAD_SIZE, rows), bf16),
            pltpu.VMEM((kv_rows, 2 * HEAD_SIZE), bf16),
            pltpu.VMEM((slots * tokens, HEAD_SIZE), bf16),
            pltpu.VMEM((slots * tokens, HEAD_SIZE), bf16),
            pltpu.VMEM((HEAD_SIZE, slots * tokens), bf16),
            pltpu.VMEM((HEAD_SIZE, slots * tokens), bf16),
            pltpu.VMEM((slots * tokens, rows), f32),
            pltpu.VMEM((slots, 1, rows), f32),
            pltpu.VMEM((HEAD_SIZE, rows), f32),
            pltpu.VMEM((kv_rows, 2 * HEAD_SIZE), f32),
        ],
    )
    out_shape = jax.ShapeDtypeStruct((docs * length, width), bf16)
    return pl.pallas_call(
        functools.partial(
            attention_kernel, group, 1.0 / math.sqrt(HEAD_SIZE), chunk, len(kv_blocks), parts, images
        ),
        grid_spec=grid_spec,
        out_shape=[out_shape, out_shape, *grad_shapes],
        compiler_params=pltpu.CompilerParams(
            vmem_limit_bytes=(12 << 20) + 16 * kv_rows * 2 * HEAD_SIZE + 24 * length * span
        ),
        cost_estimate=pl.CostEstimate(
            flops=12 * docs * length * width * slots * tokens,
            bytes_accessed=8 * docs * length * width + 5 * kv_rows * kv_cols,
            transcendentals=docs * length * width // HEAD_SIZE * slots * tokens,
        ),
        name="attention",
    )(pos, starts, bases, both, both, *kv_blocks)


def whole_call(kernel, out_shape, args, flops, name, scalar=None):
    vmem = pl.BlockSpec(memory_space=pltpu.VMEM)
    smem = pl.BlockSpec(memory_space=pltpu.SMEM)
    scalars = [] if scalar is None else [scalar.reshape(-1).astype(jnp.int32)]
    moved = sum(a.size * a.dtype.itemsize for a in (*args, *out_shape))
    return pl.pallas_call(
        kernel,
        out_shape=out_shape,
        in_specs=[smem] * len(scalars) + [vmem] * len(args),
        out_specs=[vmem] * len(out_shape),
        compiler_params=pltpu.CompilerParams(vmem_limit_bytes=16 * 1024 * 1024),
        cost_estimate=pl.CostEstimate(flops=flops, bytes_accessed=moved, transcendentals=0),
        name=name,
    )(*scalars, *args)


def in_order(core, own, other):
    return jnp.where(core == 0, own, other), jnp.where(core == 0, other, own)


def project(seen, weights, core):
    count = len(weights)
    tokens, features = seen[0][0].shape
    width = weights[0][0].shape[1] // 2

    def kernel(core_ref, *refs):
        outs = refs[4 * count :]
        totals = [None, None]
        for y in range(count):
            own, other = refs[2 * count + 2 * y : 2 * count + 2 * y + 2]
            w = jnp.concatenate(in_order(core_ref[0], own[...], other[...]), 0)
            for r in range(2):
                term = jnp.dot(refs[r * count + y][...], w, preferred_element_type=f32)
                totals[r] = term if totals[r] is None else totals[r] + term
        for total, out in zip(totals, outs, strict=True):
            for h in range(width // HEAD_SIZE):
                for kind in range(2):
                    c = (2 * h + kind) * HEAD_SIZE
                    t = total[:, kind * width + h * HEAD_SIZE :][:, :HEAD_SIZE]
                    out[:, c : c + HEAD_SIZE] = (t * SUM_SCALE).astype(out.dtype)

    shape = (tokens, 2 * width)
    shapes = [jax.ShapeDtypeStruct(shape, f32), jax.ShapeDtypeStruct(shape, f32)]
    flops = 8 * tokens * width * features * count
    args = [*seen[0], *seen[1], *(w for pair in weights for w in pair)]
    return whole_call(kernel, shapes, args, flops, "project", core)


def total_of(refs):
    total = refs[0][...]
    for ref in refs[1:]:
        total = total + ref[...].astype(f32)
    return total


def norm_forward(high, low, gain, core, halves):
    terms = [*high, *low]

    def kernel(core_ref, *refs):
        gain_ref, pre_ref = refs[len(terms) : len(terms) + 2]
        outs = refs[len(terms) + 2 :]
        total = total_of(refs[: len(terms)]) * (1.0 / SUM_SCALE)
        pre_ref[...] = total
        blocks = []
        for c in range(0, total.shape[1], 2 * HEAD_SIZE):
            blocks.append(key_norm(total[:, c : c + HEAD_SIZE], gain_ref[...]).astype(bf16))
            blocks.append(total[:, c + HEAD_SIZE : c + 2 * HEAD_SIZE].astype(bf16))
        low = jnp.concatenate(blocks, 1)
        if halves == 2:
            half = low.shape[1] // 2
            outs[0][...], outs[1][...] = in_order(core_ref[0], low[:, :half], low[:, half:])
        else:
            outs[0][...] = low

    rows, cols = terms[0].shape
    shapes = [jax.ShapeDtypeStruct((rows, cols), f32)]
    shapes += [jax.ShapeDtypeStruct((rows, cols // halves), bf16)] * halves
    outs = whole_call(kernel, shapes, [*terms, gain], 8 * rows * cols, "norm_forward", core)
    return outs[0], outs[1:]


def sum_terms(parts):
    counts = [len(high) + len(low) for high, low in parts]
    terms = [t for high, low in parts for t in (*high, *low)]

    def kernel(*refs):
        mine_ref, theirs_ref = refs[len(terms) :]
        half, cols = mine_ref.shape[0], refs[0].shape[1]
        for p, count in enumerate(counts):
            total = total_of(refs[sum(counts[:p]) : sum(counts[:p]) + count])
            here = slice(p * cols, (p + 1) * cols)
            mine_ref[:, here] = total[:half]
            theirs_ref[:, here] = total[half:]

    rows, cols = terms[0].shape
    shapes = [jax.ShapeDtypeStruct((rows // 2, len(parts) * cols), f32)] * 2
    return whole_call(kernel, shapes, terms, rows * cols * len(terms), "sum_terms")


def norm_backward(parts, high, low, pre, gain, core):
    terms = [*parts, *high, *low]

    def kernel(core_ref, *refs):
        pre_ref, gain_ref, out_ref = refs[len(terms) :]
        if parts:
            total = jnp.concatenate(in_order(core_ref[0], refs[0][...], refs[1][...]), 1)
        else:
            total = total_of(refs[: len(terms)])
        for c in range(0, total.shape[1], 2 * HEAD_SIZE):
            k = slice(c, c + HEAD_SIZE)
            x = pre_ref[:, k]
            inverse = lax.rsqrt(jnp.mean(x * x, axis=-1, keepdims=True) + norm_epsilon)
            up = total[:, k] * gain_ref[...]
            mean = jnp.mean(up * x, axis=-1, keepdims=True)
            out_ref[:, k] = (inverse * (up - x * (inverse * inverse * mean))).astype(bf16)
            v = slice(c + HEAD_SIZE, c + 2 * HEAD_SIZE)
            out_ref[:, v] = total[:, v].astype(bf16)

    shapes = [jax.ShapeDtypeStruct(pre.shape, bf16)]
    args = [*terms, pre, gain]
    return whole_call(kernel, shapes, args, 12 * pre.size, "norm_backward", core)[0]


def place_columns(pieces, width, places):
    arrays = list({id(a): a for a, _, _ in pieces}.values())
    index = {id(a): i for i, a in enumerate(arrays)}
    rows = min(a.shape[0] for a in arrays)

    def kernel(place_ref, *refs):
        for i, (a, row, col) in enumerate(pieces):
            to = pl.ds(pl.multiple_of(place_ref[i] * width, width), width)
            refs[-1][:, to] = refs[index[id(a)]][row : row + rows, col : col + width]

    shapes = [jax.ShapeDtypeStruct((rows, len(pieces) * width), arrays[0].dtype)]
    return whole_call(kernel, shapes, arrays, 0, "place_columns", places)[0]


def weight_gradient(seen, back, core):
    count, parts = len(seen), len(back)

    def kernel(core_ref, *refs):
        mine_ref, theirs_ref = refs[-2:]
        half, cols = mine_ref.shape[0], refs[count].shape[1]
        for p in range(parts):
            total = None
            for a, b in zip(refs[:count], refs[count * (p + 1) : count * (p + 2)], strict=True):
                term = lax.dot_general(
                    a[...], b[...], (((0,), (0,)), ((), ())), preferred_element_type=f32
                )
                total = term if total is None else total + term
            here = slice(p * cols, (p + 1) * cols)
            mine, theirs = in_order(core_ref[0], total[:half], total[half:])
            mine_ref[:, here] = mine
            theirs_ref[:, here] = theirs

    half, cols = seen[0].shape[1] // 2, back[0][0].shape[1] * parts
    shapes = [jax.ShapeDtypeStruct((half, cols), f32)] * 2
    flops = 4 * half * cols * count * seen[0].shape[0]
    args = [*seen, *(b for part in back for b in part)]
    return whole_call(kernel, shapes, args, flops, "weight_gradient", core)


def split_heads(parts, index):
    ys = len(parts[0])
    rows, cols = parts[0][0][0].shape
    args = [t for part in parts for block in part for t in block]

    def kernel(index_ref, *refs):
        outs = refs[-2:]

        def place(order):
            it = iter(refs)
            for p, part in enumerate(parts):
                for block, to in zip(part, order, strict=True):
                    terms = [next(it)[...].astype(f32) for _ in block]
                    total = sum(terms[1:], terms[0])
                    for c in range(0, cols, HEAD_SIZE):
                        h = (to * len(parts) + p) * (cols // 2)
                        h += c // (2 * HEAD_SIZE) * HEAD_SIZE
                        out = outs[c // HEAD_SIZE % 2]
                        out[:, h : h + HEAD_SIZE] = total[:, c : c + HEAD_SIZE]

        if ys == 2:
            for i in range(2):
                pl.when(index_ref[0] == i)(functools.partial(place, (i, 1 - i)))
        else:
            place(range(ys))

    shapes = [jax.ShapeDtypeStruct((rows, ys * len(parts) * cols // 2), f32)] * 2
    return whole_call(kernel, shapes, args, 0, "split_heads", index)


def shards(
    vision,
    key_projection_weight,
    value_projection_weight,
    key_gain,
    queries,
    out_grad,
    image_ids,
    image_counts,
    image_starts,
):
    dp = lax.axis_size("dp")
    sp = lax.axis_size("sp")
    levels = dp // 4
    d = lax.axis_index("dp")
    s = lax.axis_index("sp")
    z, x, core = d // 4, (d // 2) % 2, d % 2
    tokens = vision.shape[0] * vision.shape[1]
    own_vision = vision.reshape(tokens, vision.shape[2])
    heads = KEY_VALUE_HEADS // sp
    rows_here = key_projection_weight.shape[0]

    keys = split_y(key_projection_weight, 1)
    values = split_y(value_projection_weight, 1)
    weights = exchange_y(
        [jnp.concatenate(pair, 1) for pair in zip(keys, values, strict=True)]
    )
    weights = [(w, swap_core(w)) for w in weights]

    order = [*range(1, levels), 0]
    pieces = {}
    for j in order:
        for r in range(2):
            chip = (z + j) % levels * 2 + (x ^ r)
            piece = lax.dynamic_slice_in_dim(own_vision, chip * 2 * rows_here, 2 * rows_here, 1)
            if j > 1:
                piece = after(piece, pieces[j - 1, r])
            pieces[j, r] = piece if j == 0 and r == 0 else shift_chip(piece, j, r)
    seen = [None] * (2 * levels)
    moved = [weights[-1][0]]
    terms = [None] * levels
    for n, j in enumerate(order):
        for r in range(2):
            piece = pieces[j, r]
            if len(moved) > 1:
                piece = after(piece, moved[-2])
            seen[2 * j + r] = gather_y(piece)
            moved.append(seen[2 * j + r][-1])
        terms[j] = project(seen[2 * j : 2 * j + 2], weights, core)

    halves = 2 if heads % 2 == 0 else 1
    queries, out_grad = after(queries, moved[-1]), after(out_grad, moved[-1])
    queries, out_grad = split_y(queries[0], 1), split_y(out_grad[0], 1)
    both = exchange_y([jnp.concatenate(pair, 1) for pair in zip(queries, out_grad, strict=True)])
    both = jnp.concatenate(both, 0)
    length = both.shape[0]
    if halves == 2:
        half = both.shape[1] // 4
        cuts = [
            jnp.concatenate(
                [
                    lax.dynamic_slice_in_dim(both, (2 * kind + (core ^ c)) * half, half, 1)
                    for kind in range(2)
                ],
                1,
            )
            for c in range(2)
        ]
        both = jnp.concatenate((cuts[0], swap_core(cuts[1])), 0)

    gain = key_gain.reshape(1, HEAD_SIZE)
    high, low = reduce_chips([t[0] for t in terms], [t[1].astype(f16) for t in terms], levels, f16)
    total = sum([a.astype(f32) for a in low], high[0])
    pre, pairs = norm_forward([total], [], gain, core, halves)
    block = pairs[0]
    if halves == 2:
        block = jnp.concatenate((block, swap_core(pairs[1])), 0)
    if halves == 2:
        column = gather_chips(block, levels)
        kv_blocks = column[::2] + column[1::2]
    else:
        column = gather_chips(block, levels)
        kv_blocks = [*column, swap_core(jnp.concatenate(column, 0))]

    ids = image_ids[0].astype(jnp.int32)
    slot = jnp.arange(ids.shape[0], dtype=jnp.int32)
    first = jnp.where(slot == 0, -1, image_starts[0])
    first = jnp.where(slot < image_counts[0], first, 1 << 30)
    before = (first[None, :] < first[:, None]) | (
        (first[None, :] == first[:, None]) & (slot[None, :] < slot[:, None])
    )
    rank = jnp.sum(before.astype(jnp.int32), axis=1)
    turn = (rank[None, :] == slot[:, None]).astype(jnp.int32)
    table = jnp.sum(turn[None] * jnp.stack((ids, first))[:, None, :], axis=2)[None]
    if halves == 2:
        table = jnp.concatenate((table, swap_core(table)), 0)
    ids, first = table[:, 0], table[:, 1]
    level, far, mate = (z - ids // 4) % levels, x ^ (ids // 2 % 2), core ^ (ids % 2)
    if halves == 2:
        place = (far * levels + level) * 2 + mate
    else:
        place = (mate * levels + level) * 2 + far
    local = length // sp
    at = jnp.arange(length // TILE, dtype=jnp.int32) * TILE
    if sp == 2:
        at = (at + s * local) % length
    attended, grad_query, *blocks = attention(both, kv_blocks, 1, place, first, at)

    width = attended.shape[1]
    sources = [(attended, 0), (grad_query, 0)]
    if halves == 2:
        theirs = swap_core(jnp.concatenate((attended[length:], grad_query[length:]), 1))
        sources += [(theirs, 0), (theirs, width)]
    got = exchange_y(
        [
            jnp.concatenate(
                [a[y * local : (y + 1) * local, c : c + width] for a, c in sources], 1
            )
            for y in range(sp)
        ]
    )
    pieces = [[], []]
    for y in range(sp):
        for i, (a, c) in enumerate(sources):
            own = y == 0 and sp == 2
            pieces[i % 2].append((a, 0, c) if own else (got[y], 0, i * width))
    ys = [s ^ y if sp == 2 else y for y in range(sp)]
    places = jnp.stack([y * halves + (core ^ c) * (halves - 1) for y in ys for c in range(halves)])
    attended_out, query_out = [place_columns(p, width, places) for p in pieces]

    keeps, sends = blocks[:levels], blocks[levels:]
    if halves == 1:
        sums = [k + swap_core(a).astype(f32) for k, a in zip(keeps, sends, strict=True)]
        keeps = [a[:tokens] for a in sums]
        sends = [a[tokens:].astype(bf16) for a in sums]
        high, low = reduce_chips(keeps, sends, levels)
        back = norm_backward([], high, low, pre, gain, core)
    else:
        totals = [reduce_chips(keeps, sends, levels)]
        mine, theirs = sum_terms(totals)
        back = norm_backward((mine, swap_core(theirs)), [], [], pre, gain, core)
    back = after(back, *got)
    back = [gather_chips(b, levels) for b in jnp.split(back, halves, axis=1)]

    for p in range(len(back) - 1):
        back[p][0] = after(back[p][0], back[p + 1][1], *back[p + 1][2::2])
    grads = []
    for part in back:
        if grads:
            part = [after(part[0], *(a for y in grads[-1] for a in y)), *part[1:]]
        sent = []
        for y in reversed(range(sp)):
            mine, theirs = weight_gradient([block[y] for block in seen], [part], core)
            other = swap_core(theirs)
            if y > 0 or sp > 2:
                sent.append((mine + other).astype(bf16))
        if sp == 2:
            grads.append([(mine, other), (swap_y(sent[0]),)])
        else:
            grads.append([(a,) for a in exchange_y(sent[::-1])])
    grad_key, grad_value = split_heads(grads, s)
    return attended_out[None], query_out[None], grad_key, grad_value


def solution(mesh):
    return jax.shard_map(
        shards,
        mesh=mesh,
        in_specs=(
            P("dp", None, "sp"),
            P(("sp", "dp"), None),
            P(("sp", "dp"), None),
            P(),
            P("dp", "sp", None),
            P("dp", "sp", None),
            P("dp", None),
            P("dp"),
            P("dp", None),
        ),
        out_specs=(
            P("dp", "sp", None),
            P("dp", "sp", None),
            P(("sp", "dp"), None),
            P(("sp", "dp"), None),
        ),
        check_vma=False,
    )
```
